32 devices in a mesh: depth: 8 (over z, y), tile: 4 (over x, core).
Axes of the slice: x: 2, y: 2, z: 4, core: 2. Of those that a mesh axis runs over, the one named last changes fastest.
Arguments:
- ensemble: bfloat16 [64, 8, 64, 8192], P('tile', None, 'depth'), may hold values from -8 to 8
- active: int32 [8, 64], P('depth'), may hold values from 0 to 1, as said below
- depth_rank: int32 [8], replicated, may hold values from 0 to 7, as said below
Outputs:
- picture: float32 [4, 4, 65536], P(None, 'tile', 'depth')
The draws below stay inside these ranges and needn't reach their ends.
Inputs may be any that keep to these rules, and one draw needn't show every extreme that they name: Every slab has exactly 32 active bricks. depth_rank[s] = s XOR k for one integer k.
All inputs are finite; a program needn't handle non-finite values.
Results may differ from the reference program's by a relative error of at most 0.0003.
Values may be sent and summed in bfloat16 or wider, within the bound.
A program may use at most 128 MiB of HBM per device.

```python
import jax
import jax.numpy as jnp
from jax import lax

MEMBERS = 64
BPT = 16
BZ = 2
PIXB = 4096
CELLS = 8192
SLABS = 8
BRICKS = 64
ACTIVE = 32
N_TILE = 4


def draw_ensemble(key, part):
    cell_base = jax.random.normal(jax.random.fold_in(key, 11), (1, SLABS, BRICKS, CELLS), jnp.float32)
    noise_key = jax.random.fold_in(key, 12)
    member_noise = jax.random.normal(noise_key, (MEMBERS, SLABS, BRICKS, CELLS), jnp.float32)
    values = 1.2 * cell_base + 0.7 * member_noise
    return jnp.clip(values, -8.0, 8.0).astype(jnp.bfloat16)


def draw_active(key, part):
    noise_ints = jax.random.randint(jax.random.fold_in(key, 31), (SLABS, BRICKS), 0, 1000)
    tile_weight = jax.random.randint(jax.random.fold_in(key, 32), (SLABS, BRICKS // BPT), 0, 4)
    tile_owner = jnp.arange(BRICKS, dtype=jnp.int32) // BPT
    tile_bias = jnp.take(tile_weight, tile_owner, axis=1)
    scores = (noise_ints + 400 * tile_bias) * BRICKS + jnp.arange(BRICKS, dtype=jnp.int32)[None, :]
    top_index = lax.top_k(scores, ACTIVE)[1]
    picked = jnp.zeros((SLABS, BRICKS), jnp.int32)
    return picked.at[jnp.arange(SLABS, dtype=jnp.int32)[:, None], top_index].set(1).astype(jnp.int32)


def draw_depth_rank(key, part):
    flip_mask = jax.random.randint(jax.random.fold_in(key, 21), (), 0, SLABS)
    return jnp.bitwise_xor(jnp.arange(SLABS, dtype=jnp.int32), flip_mask).astype(jnp.int32)


def setup_inputs(seed: int = 0) -> dict:
    streams_of = jax.random.split(jax.random.key(seed), 4)
    return {
        "ensemble": draw_ensemble(jax.random.fold_in(streams_of[3], 71), 0),
        "active": draw_active(jax.random.fold_in(streams_of[3], 71), 0),
        "depth_rank": draw_depth_rank(jax.random.fold_in(streams_of[3], 71), 0),
    }


SHARPNESS = 4.0
ISOVALUE = 0.25
DENSITY = 0.35

def illuminate(mean_field, variance, above_prob):
    spread = jnp.sqrt(variance + 1e-06)
    depth_sum = jnp.cumsum(above_prob, axis=-2)
    transmit = jnp.exp(-DENSITY * (depth_sum - above_prob))
    weight = transmit * (1.0 - jnp.exp(-DENSITY * above_prob))
    red_sum = lax.optimization_barrier(jnp.sum(weight * jax.nn.sigmoid(2.0 * mean_field), axis=-2))
    green_sum = lax.optimization_barrier(jnp.sum(weight * (spread / (1.0 + spread)), axis=-2))
    blue_sum = lax.optimization_barrier(jnp.sum(weight * above_prob, axis=-2))
    opacity = 1.0 - jnp.exp(-DENSITY * depth_sum[..., -1, :])
    return jnp.stack([red_sum, green_sum, blue_sum, opacity])

def render_members(samples):
    mean_field = lax.optimization_barrier(jnp.mean(samples, axis=0))
    variance = lax.optimization_barrier(jnp.mean((samples - mean_field) ** 2, axis=0))
    above_prob = lax.optimization_barrier(jnp.mean(jax.nn.sigmoid(SHARPNESS * (samples - ISOVALUE)), axis=0))
    return illuminate(mean_field, variance, above_prob)

def reference(ensemble, active, depth_rank):

    def one_slab(slab):
        brick_block = lax.dynamic_index_in_dim(ensemble, slab, 1, keepdims=False)
        samples = brick_block.astype(jnp.float32).reshape(MEMBERS, BRICKS, BZ, PIXB)
        flags_here = lax.dynamic_index_in_dim(active, slab, 0, keepdims=False).astype(jnp.float32)
        shaded = render_members(samples) * flags_here[None, :, None]
        return shaded.reshape(4, N_TILE, BPT * PIXB)
    layers = lax.map(one_slab, jnp.arange(SLABS, dtype=jnp.int32))
    ranking = jnp.argsort(depth_rank).astype(jnp.int32)

    def advance(result, slab):
        return (result + (1.0 - result[3:4]) * layers[slab], None)
    picture, _ = lax.scan(advance, jnp.zeros((4, N_TILE, BPT * PIXB), jnp.float32), ranking)
    return picture
```

```python
import functools

import jax
import jax.numpy as jnp
from jax import lax
from jax.experimental import pallas as pl
from jax.experimental.pallas import tpu as pltpu
from jax.sharding import PartitionSpec as P

BZ = 2
CORES = 2
SHARPNESS = 4.0
ISOVALUE = 0.25
DENSITY = 0.35
FIELD_MAX = 8.0
CODE_MAX = 65535.0
MEAN_STEP = 2.0 * FIELD_MAX / CODE_MAX
ROOT_STEP = FIELD_MAX**0.5 / CODE_MAX
PROB_STEP = 1.0 / CODE_MAX
LANES = 256


def fourth_root(x):
    return jnp.sqrt(jnp.sqrt(x))


def to_code(x, step):
    return jnp.clip(x * (1.0 / step) + 0.5, 0.0, CODE_MAX).astype(jnp.int32)


def pair(low, high):
    return low | (high << 16)


def unpair(word):
    low = word & 0xFFFF
    high = lax.shift_right_logical(word, jnp.full_like(word, 16))
    return low.astype(jnp.float32), high.astype(jnp.float32)


def kernel(
    geo, ens, active, rank, out,
    held, abuf, bbuf, sibling, own, xsend, xrecv, flags, layers, rows,
    load_sem, asend_sem, arecv_sem, xsend_sem, xrecv_sem, fsend_sem, frecv_sem, osend_sem, orecv_sem, local_sem,
):
    slabs, members, bricks, pixels, depth_n, tile_n, per_tile = geo
    chips = tile_n // CORES
    width = pixels // tile_n
    lanes = min(LANES, width)
    chunks = width // lanes
    per_out = per_tile // depth_n
    d = lax.axis_index("depth")
    t = lax.axis_index("tile")
    x = t // CORES
    core = t % CORES

    def load(s):
        return pltpu.make_async_copy(ens.at[:, s], held.at[s], load_sem.at[s])

    for s in range(slabs):
        load(s).start()

    first = d * bricks
    goal_tile = first // per_tile
    goal_depth = (first % per_tile) // per_out
    my_first = t * per_tile + d * per_out
    source_depth = my_first // bricks
    same = source_depth == d
    barrier = pltpu.get_barrier_semaphore()

    def greet(depth, tile):
        pl.semaphore_signal(
            barrier, inc=1, device_id=(depth, tile), device_id_type=pl.DeviceIdType.MESH
        )

    greet(d, x * CORES + 1 - core)
    for j in range(1, chips):
        greet(d, ((x + j) % chips) * CORES + core)
    for j in range(1, depth_n):
        greet((d + j) % depth_n, t)
    goals = bricks // per_out
    for u in range(goals):
        @pl.when(jnp.logical_not(jnp.logical_and(goal_depth + u == d, goal_tile == t)))
        def _():
            greet(goal_depth + u, goal_tile)
    for u in range(tile_n):
        @pl.when(jnp.logical_not(jnp.logical_and(same, t == u)))
        def _():
            greet(source_depth, jnp.int32(u))

    def partial(s, side, store):
        def step(i, carry):
            region = i // chunks
            base = (region // BZ * CORES + side) * width + region % BZ * pixels
            column = pl.multiple_of(base + i % chunks * lanes, lanes)
            samples = [held[s, m, :, pl.ds(column, lanes)].astype(jnp.float32) for m in range(members)]
            total = samples[0]
            for v in samples[1:]:
                total = total + v
            mean = total * (1.0 / members)
            square = None
            above = None
            for v in samples:
                c = v - mean
                c = c * c
                h = jnp.tanh(v * (0.5 * SHARPNESS) - 0.5 * SHARPNESS * ISOVALUE)
                square = c if square is None else square + c
                above = h if above is None else above + h
            at = pl.ds(pl.multiple_of(i * lanes, lanes), lanes)
            store(0, at, mean)
            store(1, at, square * (1.0 / members))
            store(2, at, above * (0.5 / members) + 0.5)
            return carry

        lax.fori_loop(0, chips * BZ * chunks, step, 0)

    def store_a(s):
        def store(q, at, value):
            abuf[s, q, :, at] = value
        return store

    def store_b(q, at, value):
        bbuf[q, :, at] = value

    def to_sibling(s):
        return pltpu.make_async_remote_copy(
            src_ref=abuf.at[s], dst_ref=sibling.at[s],
            send_sem=asend_sem.at[s], recv_sem=arecv_sem.at[s],
            device_id=(d, x * CORES + 1 - core), device_id_type=pl.DeviceIdType.MESH,
        )

    def to_chip(s, j):
        return pltpu.make_async_remote_copy(
            src_ref=xsend.at[s, j - 1], dst_ref=xrecv.at[s, j - 1],
            send_sem=xsend_sem.at[s, j - 1], recv_sem=xrecv_sem.at[s, j - 1],
            device_id=(d, (x + j) % chips * CORES + core), device_id_type=pl.DeviceIdType.MESH,
        )

    def to_depth(j):
        return pltpu.make_async_remote_copy(
            src_ref=active, dst_ref=flags.at[d],
            send_sem=fsend_sem.at[j - 1], recv_sem=frecv_sem.at[j - 1],
            device_id=((d + j) % depth_n, t), device_id_type=pl.DeviceIdType.MESH,
        )

    def from_depth(j):
        return pltpu.make_async_remote_copy(
            src_ref=active, dst_ref=flags.at[(d + depth_n - j) % depth_n],
            send_sem=fsend_sem.at[j - 1], recv_sem=frecv_sem.at[j - 1],
            device_id=((d + j) % depth_n, t), device_id_type=pl.DeviceIdType.MESH,
        )

    def merged(s, at):
        ma, va, pa = (bbuf[q, :, at] for q in range(3))
        mb, vb, pb = (sibling[s, q, :, at] for q in range(3))
        gap = ma - mb
        return (ma + mb) * 0.5, (va + vb) * 0.5 + gap * gap * 0.25, (pa + pb) * 0.5

    def combine(s):
        for j in list(range(1, chips)) + [0]:
            other = (x + j) % chips

            def step(i, carry, j=j, other=other):
                at = pl.ds(pl.multiple_of(i * lanes, lanes), lanes)
                found = []
                for z in range(BZ):
                    base = (other * BZ + z) * width + i * lanes
                    found.append(merged(s, pl.ds(pl.multiple_of(base, lanes), lanes)))
                if j == 0:
                    for z in range(BZ):
                        for q in range(3):
                            own[s, z * 3 + q, :, at] = found[z][q]
                else:
                    (m0, v0, p0), (m1, v1, p1) = found
                    xsend[s, j - 1, 0, :, at] = pair(
                        to_code(m0 + FIELD_MAX, MEAN_STEP), to_code(m1 + FIELD_MAX, MEAN_STEP)
                    )
                    xsend[s, j - 1, 1, :, at] = pair(
                        to_code(fourth_root(v0), ROOT_STEP), to_code(fourth_root(v1), ROOT_STEP)
                    )
                    xsend[s, j - 1, 2, :, at] = pair(
                        to_code(fourth_root(p0), PROB_STEP), to_code(fourth_root(p1), PROB_STEP)
                    )
                return carry

            lax.fori_loop(0, chunks, step, 0)
            if j:
                to_chip(s, j).start()

    total_bricks = active.shape[1]

    def finalize(s):
        for j in range(1, chips):
            to_chip(s, j).wait_recv()
        row = flags[s]
        lane = lax.broadcasted_iota(jnp.int32, (bricks, total_bricks), 1)
        brick = lax.broadcasted_iota(jnp.int32, (bricks, total_bricks), 0)
        picked = jnp.where(lane == brick + first, row.astype(jnp.float32), 0.0)
        shown = jnp.sum(picked, axis=1, keepdims=True)

        def step(i, carry):
            at = pl.ds(pl.multiple_of(i * lanes, lanes), lanes)
            means, variances, probs = ([[own[s, z * 3 + q, :, at]] for z in range(BZ)] for q in range(3))
            for j in range(chips - 1):
                for z, code in enumerate(unpair(xrecv[s, j, 0, :, at])):
                    means[z].append(code * MEAN_STEP - FIELD_MAX)
                for z, code in enumerate(unpair(xrecv[s, j, 1, :, at])):
                    root = code * ROOT_STEP
                    variances[z].append(root * root * (root * root))
                for z, code in enumerate(unpair(xrecv[s, j, 2, :, at])):
                    root = code * PROB_STEP
                    probs[z].append(root * root * (root * root))
            mean, spread, prob = [], [], []
            for z in range(BZ):
                m = sum(means[z][1:], means[z][0]) * (1.0 / chips)
                v = sum(variances[z][1:], variances[z][0])
                for part in means[z]:
                    v = v + (part - m) * (part - m)
                mean.append(m)
                spread.append(jnp.sqrt(v * (1.0 / chips) + 1e-06))
                prob.append(sum(probs[z][1:], probs[z][0]) * (1.0 / chips))
            clear = [jnp.exp(-DENSITY * p) for p in prob]
            weight = [1.0 - clear[0], clear[0] * (1.0 - clear[1])]
            red = green = blue = 0.0
            for z in range(BZ):
                red = red + weight[z] * (0.5 + 0.5 * jnp.tanh(mean[z]))
                green = green + weight[z] * (spread[z] / (1.0 + spread[z]))
                blue = blue + weight[z] * prob[z]
            opacity = 1.0 - jnp.exp(-DENSITY * (prob[0] + prob[1]))
            for c, value in enumerate((red, green, blue, opacity)):
                layers[s, c, :, at] = value * shown
            return carry

        lax.fori_loop(0, chunks, step, 0)

    load(0).wait()
    partial(0, 1 - core, store_a(0))
    pl.semaphore_wait(
        barrier, chips + depth_n - 1 + goals + tile_n - 2 * same.astype(jnp.int32)
    )
    to_sibling(0).start()
    for j in range(1, depth_n):
        to_depth(j).start()
    mine = pltpu.make_async_copy(active, flags.at[d], local_sem.at[bricks])
    mine.start()
    mine.wait()

    def slab_step(s, carry):
        partial(s, core, store_b)

        @pl.when(s < slabs - 1)
        def _():
            load(s + 1).wait()
            partial(s + 1, 1 - core, store_a(s + 1))
            to_sibling(s + 1).start()

        to_sibling(s).wait_recv()
        combine(s)

        @pl.when(s == 0)
        def _():
            for j in range(1, depth_n):
                from_depth(j).wait_recv()

        @pl.when(s > 0)
        def _():
            finalize(s - 1)

        return carry

    lax.fori_loop(0, slabs, slab_step, 0)
    finalize(slabs - 1)

    flip = rank[0]

    def blend(i, carry):
        at = pl.ds(pl.multiple_of(i * lanes, lanes), lanes)

        def over(r, picture):
            slab = lax.bitwise_xor(r, flip)
            through = 1.0 - picture[3]
            return tuple(picture[c] + through * layers[slab, c, :, at] for c in range(4))

        picture = lax.fori_loop(0, slabs, over, tuple(jnp.zeros((bricks, lanes), jnp.float32) for _ in range(4)))
        for b in range(bricks):
            for c in range(4):
                rows[b, c : c + 1, at] = picture[c][b : b + 1, :]
        return carry

    lax.fori_loop(0, chunks, blend, 0)

    def place(tile, slot):
        return out.at[:, pl.ds(pl.multiple_of(slot * pixels + tile * width, width), width)]

    def is_self(b):
        return jnp.logical_and(goal_depth + b // per_out == d, goal_tile == t)

    def keep(b):
        return pltpu.make_async_copy(rows.at[b], place(t, b % per_out), local_sem.at[b])

    def hand(b):
        return pltpu.make_async_remote_copy(
            src_ref=rows.at[b], dst_ref=place(t, b % per_out),
            send_sem=osend_sem.at[b], recv_sem=orecv_sem.at[t, b % per_out],
            device_id=(goal_depth + b // per_out, goal_tile), device_id_type=pl.DeviceIdType.MESH,
        )

    for b in range(bricks):
        @pl.when(is_self(b))
        def _():
            keep(b).start()

        @pl.when(jnp.logical_not(is_self(b)))
        def _():
            hand(b).start()

    for b in range(bricks):
        @pl.when(is_self(b))
        def _():
            keep(b).wait()

        @pl.when(jnp.logical_not(is_self(b)))
        def _():
            hand(b).wait_send()

    for u in range(tile_n):
        @pl.when(jnp.logical_not(jnp.logical_and(same, t == u)))
        def _():
            for slot in range(per_out):
                pltpu.make_async_remote_copy(
                    src_ref=rows.at[slot], dst_ref=place(u, slot),
                    send_sem=osend_sem.at[slot], recv_sem=orecv_sem.at[u, slot],
                    device_id=(source_depth, jnp.int32(u)), device_id_type=pl.DeviceIdType.MESH,
                ).wait_recv()

    def drain(s, carry):
        to_sibling(s).wait_send()
        for j in range(1, chips):
            to_chip(s, j).wait_send()
        return carry

    lax.fori_loop(0, slabs, drain, 0)
    for j in range(1, depth_n):
        to_depth(j).wait_send()


def body(ensemble, active, depth_rank):
    tile_n = lax.axis_size("tile")
    depth_n = lax.axis_size("depth")
    members, slabs, bricks, cells = ensemble.shape
    pixels = cells // BZ
    per_tile = active.shape[1] // tile_n
    per_out = per_tile // depth_n
    chips = tile_n // CORES
    width = pixels // tile_n
    geo = (slabs, members, bricks, pixels, depth_n, tile_n, per_tile)
    f32, i32 = jnp.float32, jnp.int32
    side = chips * BZ * width
    dma = pltpu.SemaphoreType.DMA
    picture = pl.pallas_call(
        functools.partial(kernel, geo),
        out_shape=jax.ShapeDtypeStruct((4, per_out * pixels), f32),
        in_specs=[
            pl.BlockSpec(memory_space=pl.ANY),
            pl.BlockSpec(memory_space=pltpu.VMEM),
            pl.BlockSpec(memory_space=pltpu.SMEM),
        ],
        out_specs=pl.BlockSpec(memory_space=pltpu.VMEM),
        scratch_shapes=[
            pltpu.VMEM((slabs, members, bricks, cells), jnp.bfloat16),
            pltpu.VMEM((slabs, 3, bricks, side), f32),
            pltpu.VMEM((3, bricks, side), f32),
            pltpu.VMEM((slabs, 3, bricks, side), f32),
            pltpu.VMEM((slabs, 3 * BZ, bricks, width), f32),
            pltpu.VMEM((slabs, chips - 1, 3, bricks, width), i32),
            pltpu.VMEM((slabs, chips - 1, 3, bricks, width), i32),
            pltpu.VMEM((depth_n, 1, active.shape[1]), i32),
            pltpu.VMEM((slabs, 4, bricks, width), f32),
            pltpu.VMEM((bricks, 4, width), f32),
            dma((slabs,)),
            dma((slabs,)),
            dma((slabs,)),
            dma((slabs, chips - 1)),
            dma((slabs, chips - 1)),
            dma((depth_n - 1,)),
            dma((depth_n - 1,)),
            dma((bricks,)),
            dma((tile_n, per_out)),
            dma((bricks + 1,)),
        ],
        compiler_params=pltpu.CompilerParams(
            collective_id=0, has_side_effects=True, vmem_limit_bytes=56 * 1024 * 1024
        ),
    )(ensemble, active, depth_rank)
    return picture[:, None, :]


def solution(mesh):
    in_specs = (P("tile", None, "depth", None), P("depth", None), P())
    out_specs = P(None, "tile", "depth")
    return jax.shard_map(body, mesh=mesh, in_specs=in_specs, out_specs=out_specs, check_vma=False)
```

```python
import functools

import jax
import jax.numpy as jnp
from jax import lax
from jax.experimental import pallas as pl
from jax.experimental.pallas import tpu as pltpu
from jax.sharding import PartitionSpec as P

BZ = 2
CORES = 2
SHARPNESS = 4.0
ISOVALUE = 0.25
DENSITY = 0.35
FIELD_MAX = 8.0
CODE_MAX = 65535.0
MEAN_STEP = 2.0 * FIELD_MAX / CODE_MAX
ROOT_STEP = FIELD_MAX**0.5 / CODE_MAX
PROB_STEP = 1.0 / CODE_MAX
LANES = 1024
LEAD = 2
UNROLL = 1


def fourth_root(x):
    return jnp.sqrt(jnp.sqrt(x))


def to_code(x, step):
    return jnp.clip(x * (1.0 / step) + 0.5, 0.0, CODE_MAX).astype(jnp.int32)


def pair(low, high):
    return low | (high << 16)


def unpair(word):
    low = word & 0xFFFF
    high = lax.shift_right_logical(word, jnp.full_like(word, 16))
    return low.astype(jnp.float32), high.astype(jnp.float32)


def kernel(
    geo, ens, active, rank, out,
    held, afar, anear, bfar, bnear, sibfar, sibnear, own, xsend, xrecv, flags, layers, rows,
    load_sem, asend_sem, arecv_sem, xsend_sem, xrecv_sem, fsend_sem, frecv_sem, osend_sem, orecv_sem, local_sem,
):
    slabs, members, bricks, pixels, depth_n, tile_n, per_tile = geo
    chips = tile_n // CORES
    width = pixels // tile_n
    lanes = min(LANES, width)
    chunks = width // lanes
    per_out = per_tile // depth_n
    d = lax.axis_index("depth")
    t = lax.axis_index("tile")
    x = t // CORES
    core = t % CORES

    def load(s):
        return pltpu.make_async_copy(ens.at[:, s], held.at[s], load_sem.at[s])

    for s in range(slabs):
        load(s).start()

    first = d * bricks
    goal_tile = first // per_tile
    goal_depth = (first % per_tile) // per_out
    my_first = t * per_tile + d * per_out
    source_depth = my_first // bricks
    same = source_depth == d
    barrier = pltpu.get_barrier_semaphore()

    def greet(depth, tile):
        pl.semaphore_signal(
            barrier, inc=1, device_id=(depth, tile), device_id_type=pl.DeviceIdType.MESH
        )

    greet(d, x * CORES + 1 - core)
    for j in range(1, chips):
        greet(d, ((x + j) % chips) * CORES + core)
    for j in range(1, depth_n):
        greet((d + j) % depth_n, t)
    goals = bricks // per_out
    for u in range(goals):
        @pl.when(jnp.logical_not(jnp.logical_and(goal_depth + u == d, goal_tile == t)))
        def _():
            greet(goal_depth + u, goal_tile)
    for u in range(tile_n):
        @pl.when(jnp.logical_not(jnp.logical_and(same, t == u)))
        def _():
            greet(source_depth, jnp.int32(u))

    def partial(s, side, far, store):
        def step(i, carry):
            region = i // chunks
            chip = (x + 1 + region // BZ) % chips if far else x
            start = (chip * CORES + side) * width + region % BZ * pixels
            column = pl.multiple_of(start + i % chunks * lanes, lanes)
            base = held[s, 0, :, pl.ds(column, lanes)].astype(jnp.float32)
            total = square = None
            above = jnp.tanh(base * (0.5 * SHARPNESS) - 0.5 * SHARPNESS * ISOVALUE)
            for m in range(1, members):
                v = held[s, m, :, pl.ds(column, lanes)].astype(jnp.float32)
                above = above + jnp.tanh(v * (0.5 * SHARPNESS) - 0.5 * SHARPNESS * ISOVALUE)
                c = v - base
                total = c if total is None else total + c
                c = c * c
                square = c if square is None else square + c
            at = pl.ds(pl.multiple_of(i * lanes, lanes), lanes)
            shift = total * (1.0 / members)
            store(0, at, base + shift)
            store(1, at, jnp.maximum(square * (1.0 / members) - shift * shift, 0.0))
            store(2, at, above * (0.5 / members) + 0.5)
            return carry

        lax.fori_loop(0, (chips - 1 if far else 1) * BZ * chunks, step, 0, unroll=UNROLL)

    def store_a(s, far):
        target = afar if far else anear

        def store(q, at, value):
            target[s, q, :, at] = value
        return store

    def store_b(far):
        target = bfar if far else bnear

        def store(q, at, value):
            target[q, :, at] = value
        return store

    def to_sibling(s, far):
        part = 0 if far else 1
        return pltpu.make_async_remote_copy(
            src_ref=(afar if far else anear).at[s], dst_ref=(sibfar if far else sibnear).at[s],
            send_sem=asend_sem.at[part, s], recv_sem=arecv_sem.at[part, s],
            device_id=(d, x * CORES + 1 - core), device_id_type=pl.DeviceIdType.MESH,
        )

    def to_chip(s, j):
        return pltpu.make_async_remote_copy(
            src_ref=xsend.at[s, j - 1], dst_ref=xrecv.at[s, j - 1],
            send_sem=xsend_sem.at[s, j - 1], recv_sem=xrecv_sem.at[s, j - 1],
            device_id=(d, (x + j) % chips * CORES + core), device_id_type=pl.DeviceIdType.MESH,
        )

    def to_depth(j):
        return pltpu.make_async_remote_copy(
            src_ref=active, dst_ref=flags.at[d],
            send_sem=fsend_sem.at[j - 1], recv_sem=frecv_sem.at[j - 1],
            device_id=((d + j) % depth_n, t), device_id_type=pl.DeviceIdType.MESH,
        )

    def from_depth(j):
        return pltpu.make_async_remote_copy(
            src_ref=active, dst_ref=flags.at[(d + depth_n - j) % depth_n],
            send_sem=fsend_sem.at[j - 1], recv_sem=frecv_sem.at[j - 1],
            device_id=((d + j) % depth_n, t), device_id_type=pl.DeviceIdType.MESH,
        )

    def merged(s, far, at):
        b, sibling = (bfar, sibfar) if far else (bnear, sibnear)
        ma, va, pa = (b[q, :, at] for q in range(3))
        mb, vb, pb = (sibling[s, q, :, at] for q in range(3))
        gap = ma - mb
        return (ma + mb) * 0.5, (va + vb) * 0.5 + gap * gap * 0.25, (pa + pb) * 0.5

    def combine_far(s):
        for j in range(1, chips):
            def step(i, carry, j=j):
                at = pl.ds(pl.multiple_of(i * lanes, lanes), lanes)
                found = []
                for z in range(BZ):
                    base = ((j - 1) * BZ + z) * width + i * lanes
                    found.append(merged(s, True, pl.ds(pl.multiple_of(base, lanes), lanes)))
                (m0, v0, p0), (m1, v1, p1) = found
                xsend[s, j - 1, 0, :, at] = pair(
                    to_code(m0 + FIELD_MAX, MEAN_STEP), to_code(m1 + FIELD_MAX, MEAN_STEP)
                )
                xsend[s, j - 1, 1, :, at] = pair(
                    to_code(fourth_root(v0), ROOT_STEP), to_code(fourth_root(v1), ROOT_STEP)
                )
                xsend[s, j - 1, 2, :, at] = pair(
                    to_code(fourth_root(p0), PROB_STEP), to_code(fourth_root(p1), PROB_STEP)
                )
                return carry

            lax.fori_loop(0, chunks, step, 0)
            to_chip(s, j).start()

    def combine_near(s):
        def step(i, carry):
            at = pl.ds(pl.multiple_of(i * lanes, lanes), lanes)
            for z in range(BZ):
                found = merged(s, False, pl.ds(pl.multiple_of(z * width + i * lanes, lanes), lanes))
                for q in range(3):
                    own[s, z * 3 + q, :, at] = found[q]
            return carry

        lax.fori_loop(0, chunks, step, 0)

    total_bricks = active.shape[1]

    def finalize(s):
        for j in range(1, chips):
            to_chip(s, j).wait_recv()
        row = flags[s]
        lane = lax.broadcasted_iota(jnp.int32, (bricks, total_bricks), 1)
        brick = lax.broadcasted_iota(jnp.int32, (bricks, total_bricks), 0)
        picked = jnp.where(lane == brick + first, row.astype(jnp.float32), 0.0)
        shown = jnp.sum(picked, axis=1, keepdims=True)

        def step(i, carry):
            at = pl.ds(pl.multiple_of(i * lanes, lanes), lanes)
            means, variances, probs = ([[own[s, z * 3 + q, :, at]] for z in range(BZ)] for q in range(3))
            for j in range(chips - 1):
                for z, code in enumerate(unpair(xrecv[s, j, 0, :, at])):
                    means[z].append(code * MEAN_STEP - FIELD_MAX)
                for z, code in enumerate(unpair(xrecv[s, j, 1, :, at])):
                    root = code * ROOT_STEP
                    variances[z].append(root * root * (root * root))
                for z, code in enumerate(unpair(xrecv[s, j, 2, :, at])):
                    root = code * PROB_STEP
                    probs[z].append(root * root * (root * root))
            mean, spread, prob = [], [], []
            for z in range(BZ):
                m = sum(means[z][1:], means[z][0]) * (1.0 / chips)
                v = sum(variances[z][1:], variances[z][0])
                for part in means[z]:
                    v = v + (part - m) * (part - m)
                mean.append(m)
                spread.append(jnp.sqrt(v * (1.0 / chips) + 1e-06))
                prob.append(sum(probs[z][1:], probs[z][0]) * (1.0 / chips))
            clear = [jnp.exp(-DENSITY * p) for p in prob]
            weight = [1.0 - clear[0], clear[0] * (1.0 - clear[1])]
            red = green = blue = 0.0
            for z in range(BZ):
                red = red + weight[z] * (0.5 + 0.5 * jnp.tanh(mean[z]))
                green = green + weight[z] * (spread[z] / (1.0 + spread[z]))
                blue = blue + weight[z] * prob[z]
            opacity = 1.0 - jnp.exp(-DENSITY * (prob[0] + prob[1]))
            for c, value in enumerate((red, green, blue, opacity)):
                layers[s, c, :, at] = value * shown
            return carry

        lax.fori_loop(0, chunks, step, 0)

    lead = min(LEAD, slabs)

    def lead_step(s, carry):
        load(s).wait()
        partial(s, 1 - core, True, store_a(s, True))
        return carry

    lax.fori_loop(0, lead, lead_step, 0)
    pl.semaphore_wait(
        barrier, chips + depth_n - 1 + goals + tile_n - 2 * same.astype(jnp.int32)
    )
    for s in range(lead):
        to_sibling(s, True).start()
    for j in range(1, depth_n):
        to_depth(j).start()
    mine = pltpu.make_async_copy(active, flags.at[d], local_sem.at[bricks])
    mine.start()
    mine.wait()

    def far_step(s, carry):
        @pl.when(s < slabs - lead)
        def _():
            load(s + lead).wait()
            partial(s + lead, 1 - core, True, store_a(s + lead, True))
            to_sibling(s + lead, True).start()

        partial(s, core, True, store_b(True))
        to_sibling(s, True).wait_recv()
        combine_far(s)
        return carry

    lax.fori_loop(0, slabs, far_step, 0)

    def near_step(s, carry):
        partial(s, 1 - core, False, store_a(s, False))
        to_sibling(s, False).start()
        partial(s, core, False, store_b(False))
        to_sibling(s, False).wait_recv()
        combine_near(s)
        return carry

    lax.fori_loop(0, slabs, near_step, 0)

    for j in range(1, depth_n):
        from_depth(j).wait_recv()

    def finalize_step(s, carry):
        finalize(s)
        return carry

    lax.fori_loop(0, slabs, finalize_step, 0)

    flip = rank[0]

    def blend(i, carry):
        at = pl.ds(pl.multiple_of(i * lanes, lanes), lanes)

        def over(r, picture):
            slab = lax.bitwise_xor(r, flip)
            through = 1.0 - picture[3]
            return tuple(picture[c] + through * layers[slab, c, :, at] for c in range(4))

        picture = lax.fori_loop(0, slabs, over, tuple(jnp.zeros((bricks, lanes), jnp.float32) for _ in range(4)))
        for b in range(bricks):
            for c in range(4):
                rows[b, c : c + 1, at] = picture[c][b : b + 1, :]
        return carry

    lax.fori_loop(0, chunks, blend, 0)

    def place(tile, slot):
        return out.at[:, pl.ds(pl.multiple_of(slot * pixels + tile * width, width), width)]

    def is_self(b):
        return jnp.logical_and(goal_depth + b // per_out == d, goal_tile == t)

    def keep(b):
        return pltpu.make_async_copy(rows.at[b], place(t, b % per_out), local_sem.at[b])

    def hand(b):
        return pltpu.make_async_remote_copy(
            src_ref=rows.at[b], dst_ref=place(t, b % per_out),
            send_sem=osend_sem.at[b], recv_sem=orecv_sem.at[t, b % per_out],
            device_id=(goal_depth + b // per_out, goal_tile), device_id_type=pl.DeviceIdType.MESH,
        )

    for b in range(bricks):
        @pl.when(is_self(b))
        def _():
            keep(b).start()

        @pl.when(jnp.logical_not(is_self(b)))
        def _():
            hand(b).start()

    for b in range(bricks):
        @pl.when(is_self(b))
        def _():
            keep(b).wait()

        @pl.when(jnp.logical_not(is_self(b)))
        def _():
            hand(b).wait_send()

    for u in range(tile_n):
        @pl.when(jnp.logical_not(jnp.logical_and(same, t == u)))
        def _():
            for slot in range(per_out):
                pltpu.make_async_remote_copy(
                    src_ref=rows.at[slot], dst_ref=place(u, slot),
                    send_sem=osend_sem.at[slot], recv_sem=orecv_sem.at[u, slot],
                    device_id=(source_depth, jnp.int32(u)), device_id_type=pl.DeviceIdType.MESH,
                ).wait_recv()

    def drain(s, carry):
        to_sibling(s, True).wait_send()
        to_sibling(s, False).wait_send()
        for j in range(1, chips):
            to_chip(s, j).wait_send()
        return carry

    lax.fori_loop(0, slabs, drain, 0)
    for j in range(1, depth_n):
        to_depth(j).wait_send()


def body(ensemble, active, depth_rank):
    tile_n = lax.axis_size("tile")
    depth_n = lax.axis_size("depth")
    members, slabs, bricks, cells = ensemble.shape
    pixels = cells // BZ
    per_tile = active.shape[1] // tile_n
    per_out = per_tile // depth_n
    chips = tile_n // CORES
    width = pixels // tile_n
    geo = (slabs, members, bricks, pixels, depth_n, tile_n, per_tile)
    f32, i32 = jnp.float32, jnp.int32
    near = BZ * width
    far = (chips - 1) * near
    dma = pltpu.SemaphoreType.DMA
    picture = pl.pallas_call(
        functools.partial(kernel, geo),
        out_shape=jax.ShapeDtypeStruct((4, per_out * pixels), f32),
        in_specs=[
            pl.BlockSpec(memory_space=pl.ANY),
            pl.BlockSpec(memory_space=pltpu.VMEM),
            pl.BlockSpec(memory_space=pltpu.SMEM),
        ],
        out_specs=pl.BlockSpec(memory_space=pltpu.VMEM),
        scratch_shapes=[
            pltpu.VMEM((slabs, members, bricks, cells), jnp.bfloat16),
            pltpu.VMEM((slabs, 3, bricks, far), f32),
            pltpu.VMEM((slabs, 3, bricks, near), f32),
            pltpu.VMEM((3, bricks, far), f32),
            pltpu.VMEM((3, bricks, near), f32),
            pltpu.VMEM((slabs, 3, bricks, far), f32),
            pltpu.VMEM((slabs, 3, bricks, near), f32),
            pltpu.VMEM((slabs, 3 * BZ, bricks, width), f32),
            pltpu.VMEM((slabs, chips - 1, 3, bricks, width), i32),
            pltpu.VMEM((slabs, chips - 1, 3, bricks, width), i32),
            pltpu.VMEM((depth_n, 1, active.shape[1]), i32),
            pltpu.VMEM((slabs, 4, bricks, width), f32),
            pltpu.VMEM((bricks, 4, width), f32),
            dma((slabs,)),
            dma((2, slabs)),
            dma((2, slabs)),
            dma((slabs, chips - 1)),
            dma((slabs, chips - 1)),
            dma((depth_n - 1,)),
            dma((depth_n - 1,)),
            dma((bricks,)),
            dma((tile_n, per_out)),
            dma((bricks + 1,)),
        ],
        compiler_params=pltpu.CompilerParams(
            collective_id=0, has_side_effects=True, vmem_limit_bytes=56 * 1024 * 1024
        ),
    )(ensemble, active, depth_rank)
    return picture[:, None, :]


def solution(mesh):
    in_specs = (P("tile", None, "depth", None), P("depth", None), P())
    out_specs = P(None, "tile", "depth")
    return jax.shard_map(body, mesh=mesh, in_specs=in_specs, out_specs=out_specs, check_vma=False)
```
